32 devices in a mesh: section: 4 (over z), dp: 4 (over y, x), tensor: 2 (over core).
Axes of the slice: x: 2, y: 2, z: 4, core: 2. Of those that a mesh axis runs over, the one named last changes fastest.
Arguments:
- grad_hidden: bfloat16 [4, 512, 16384], P('section', None, ('dp', 'tensor')), may hold values from -6 to 6
- gate_pre: bfloat16 [4, 512, 16384], P('section', None, ('dp', 'tensor')), may hold values from -6 to 6
- up_pre: bfloat16 [4, 512, 16384], P('section', None, ('dp', 'tensor')), may hold values from -6 to 6
- w_gate: bfloat16 [4, 16384, 6144], P('section', ('dp', 'tensor')), may hold values from -0.078125 to 0.078125
- w_up: bfloat16 [4, 16384, 6144], P('section', ('dp', 'tensor')), may hold values from -0.078125 to 0.078125
- block_expert: int32 [4, 4], P('section'), may hold values from 0 to 1
Outputs:
- prev_grad: bfloat16 [4, 512, 6144], P('section', ('dp', 'tensor'))
The draws below stay inside these ranges and needn't reach their ends.
Inputs may be any that keep to these rules, and one draw needn't show every extreme that they name: block_expert[s, b] is the expert of rows b * 128 to (b + 1) * 128 - 1 of layer s.
All inputs are finite; a program needn't handle non-finite values.
Results may differ from the reference program's by a relative error of at most 0.019.
Values may be sent and summed in bfloat16 or wider, within the bound.
No kernel may reach another device: no remote copies, remote signals or barrier semaphores. Data moves between devices by JAX's collectives and lax.ppermute only.
A program may use at most 192 MiB of HBM per device.

```python
import math
import jax
import jax.numpy as jnp
import numpy as np
from jax import lax

D = 6144
F = 8192
EXPERTS = 2
BLOCK = 128
SECTIONS = 4
BLOCKS = 4
ROWS = 512
HID_DEV = 2048


def touch_ends(values, key, smallest, top_value):
    index_at = [jax.random.randint(jax.random.fold_in(key, axis), (), 0, length) for axis, length in enumerate(values.shape)]
    main_axis = values.shape.index(max(values.shape))
    neighbour = index_at[:main_axis] + [(index_at[main_axis] + 1) % values.shape[main_axis]] + index_at[main_axis + 1:]
    return values.at[tuple(index_at)].set(smallest).at[tuple(neighbour)].set(top_value)


def with_spikes(entries, rng, source, target, parts, factor):
    owner, partner = [(jnp.arange(entries.shape[axis_at]) // (entries.shape[axis_at] // parts)).reshape([-1 if axis == axis_at else 1 for axis in range(entries.ndim)]) for axis_at in (source, target)]
    chosen = jax.random.permutation(rng, parts)[partner]
    strong = (owner == chosen) | (owner == (partner + parts // 2) % parts)
    return jnp.where(strong, factor * entries, entries)


def level_of(key, shape, split, low, largest):
    def one(position, shards_of):
        steps = jax.random.uniform(jax.random.fold_in(jax.random.fold_in(key, 6), position), (shards_of,), jnp.float32, low / len(split), largest / len(split))
        return jnp.repeat(jnp.exp(steps), shape[position] // shards_of).reshape((-1,) + (1,) * (len(shape) - position - 1))

    loudness = one(*split[0])
    for cut in split[1:]:
        loudness = loudness * one(*cut)
    return loudness


def rank_table(amount, skew):
    weights = [(1 << 20) // math.isqrt(grade ** skew) + 1 for grade in range(1, amount + 1)]
    deviation = 1 + sum(weights) // (1 << 30)
    return np.cumsum(np.array([max(1, weight // deviation) for weight in weights]))


def skewed_ids(rng, extent, number_of, slope):
    listing = rank_table(number_of, slope)
    pick = jax.random.randint(jax.random.fold_in(rng, 1), extent, 0, int(listing[number_of - 1]))
    grade = jnp.searchsorted(jnp.asarray(listing, jnp.int32), pick, side="right")
    return jax.random.permutation(jax.random.fold_in(rng, 2), number_of)[grade].astype(jnp.int32)


def gaussian(key, shape, deviation, most, pieces=(), held_as=jnp.bfloat16):
    values = deviation * jax.random.normal(key, shape, jnp.float32)
    if pieces:
        values = values * level_of(key, shape, pieces, -0.22, 0.18)
    return jnp.clip(values, -most, most).astype(held_as)


def heavy_noise(stream_key, shape, deviation, bound, cuts, heavy, kind=jnp.bfloat16):
    drawn = deviation * jax.random.normal(stream_key, shape, jnp.float32)
    if cuts:
        drawn = drawn * level_of(stream_key, shape, cuts, -0.22, 0.18)
    return jnp.clip(with_spikes(drawn, jax.random.fold_in(stream_key, 3), *heavy), -bound, bound).astype(kind)


def setup_inputs(seed: int = 0) -> dict:
    seeds = jax.random.split(jax.random.key(seed), 7)
    grad_hidden = heavy_noise(seeds[0], (SECTIONS, ROWS, EXPERTS * F), 1.0, 6.0, ((0, 4), (2, 8)), (2, 1, 8, 2.0))
    gate_pre = gaussian(seeds[1], (SECTIONS, ROWS, EXPERTS * F), 1.0, 6.0, ((0, 4), (2, 8)))
    up_pre = gaussian(seeds[2], (SECTIONS, ROWS, EXPERTS * F), 1.0, 6.0, ((0, 4), (2, 8)))
    w_gate = gaussian(seeds[3], (SECTIONS, EXPERTS * F, D), D ** -0.5, 0.078125, ((0, 4), (1, 8)))
    w_up = gaussian(seeds[4], (SECTIONS, EXPERTS * F, D), D ** -0.5, 0.078125, ((0, 4), (1, 8)))
    block_expert = touch_ends(skewed_ids(seeds[5], (SECTIONS, BLOCKS), EXPERTS, 2), jax.random.fold_in(seeds[5], 3), 0, EXPERTS - 1).astype(jnp.int32)
    return dict(grad_hidden=grad_hidden, gate_pre=gate_pre, up_pre=up_pre, w_gate=w_gate, w_up=w_up, block_expert=block_expert)


def reference(grad_hidden, gate_pre, up_pre, w_gate, w_up, block_expert):
    groups = F // HID_DEV

    def one_section(items):
        grad_all, gate_all, up_all, gate_weight, up_weight, layout = items

        def one_block(block_id):
            expert_id = layout[block_id]
            first_row = (block_id * BLOCK).astype(jnp.int32)
            first_col = (expert_id * F).astype(jnp.int32)
            grad_rows = lax.dynamic_slice_in_dim(lax.dynamic_slice_in_dim(grad_all, first_row, BLOCK, 0), first_col, F, 1)
            gate_rows = lax.dynamic_slice_in_dim(lax.dynamic_slice_in_dim(gate_all, first_row, BLOCK, 0), first_col, F, 1)
            up_rows = lax.dynamic_slice_in_dim(lax.dynamic_slice_in_dim(up_all, first_row, BLOCK, 0), first_col, F, 1)
            gate_mat = lax.dynamic_slice_in_dim(gate_weight, first_col, F, 0)
            up_mat = lax.dynamic_slice_in_dim(up_weight, first_col, F, 0)
            gate_f = gate_rows.astype(jnp.float32)
            sig_gate = jax.nn.sigmoid(gate_f)
            grad_f = grad_rows.astype(jnp.float32)
            grad_gate = (grad_f * up_rows.astype(jnp.float32) * sig_gate * (1.0 + gate_f * (1.0 - sig_gate))).astype(jnp.bfloat16)
            grad_up = (grad_f * gate_f * sig_gate).astype(jnp.bfloat16)
            gate_groups = grad_gate.astype(jnp.float32).reshape(BLOCK, groups, HID_DEV)
            up_groups = grad_up.astype(jnp.float32).reshape(BLOCK, groups, HID_DEV)
            gate_split = gate_mat.astype(jnp.float32).reshape(groups, HID_DEV, D)
            up_split = up_mat.astype(jnp.float32).reshape(groups, HID_DEV, D)
            terms = jnp.einsum('rpi,pid->prd', gate_groups, gate_split) + jnp.einsum('rpi,pid->prd', up_groups, up_split)
            rounded = lax.optimization_barrier(terms.astype(jnp.bfloat16)).astype(jnp.float32)
            return jnp.sum(rounded, axis=0).astype(jnp.bfloat16)

        blocks_out = lax.map(one_block, jnp.arange(BLOCKS, dtype=jnp.int32))
        return blocks_out.reshape(ROWS, D)

    input_grad = lax.map(one_section, (grad_hidden, gate_pre, up_pre, w_gate, w_up, block_expert))
    return jnp.roll(input_grad, -1, axis=0)
```

```python
import functools

import jax
import jax.numpy as jnp
from jax import lax
from jax.experimental import pallas as pl
from jax.experimental.pallas import tpu as pltpu
from jax.sharding import PartitionSpec as P

F = 8192
BLOCK = 128
HALF = BLOCK // 2
DEPTH = 3
PLAN = (2, 3, 4, 2, 1)
TURNED = False
HBM = pltpu.MemorySpace.HBM
VMEM = pltpu.MemorySpace.VMEM


def swiglu_grads(grad, gate, up):
    grad = grad.astype(jnp.float32)
    gate = gate.astype(jnp.float32)
    up = up.astype(jnp.float32)
    sig = 0.5 * jnp.tanh(0.5 * gate) + 0.5
    gated = gate * sig
    grad_gate = (grad * sig) * up * (1.0 + gate - gated)
    return grad_gate.astype(jnp.bfloat16), (grad * gated).astype(jnp.bfloat16)


def parts_of(blocks, xor):
    return [(0, 2), (2, 3), (3, 4)] if xor else [(0, blocks)]


def terms_kernel(*refs, first, prepare, waits, xor, turned):
    refs = list(refs)
    layout = refs.pop(0)
    rows = [refs.pop(0) for _ in range(3 if prepare else 1)]
    if not prepare:
        refs.pop(0)
    w_gate, w_up = refs.pop(0), refs.pop(0)
    del refs[:waits]
    ring = refs.pop(0)
    keep = refs.pop(0)
    blocks, _, width = keep.shape
    sends = [(low, high, refs.pop(0)) for low, high in parts_of(blocks, xor)]
    lhs = refs.pop(0) if prepare else rows[0]
    order, wsem = refs.pop(0), refs.pop(0)
    if prepare:
        abuf, asem = refs
    hid, columns = w_gate.shape
    depth, _, tile = ring.shape
    steps = width // tile
    ahead = 0 if prepare else 1
    wanted = steps + (1 if first + width < columns else 0)
    rank = lax.axis_index("dp")
    pair = lax.axis_index("tensor")
    mine = lax.div((rank * lax.axis_size("tensor") + pair) * hid, F)

    def block_of(mask):
        return lax.bitwise_xor(rank, mask) if xor else mask

    def slot_of(mask):
        return lax.rem(mask, 2) * 2 + lax.div(mask, 2) if turned else mask

    count = jnp.int32(0)
    for mask in range(blocks):
        owned = layout[0, block_of(mask)] == mine

        @pl.when(owned)
        def _(count=count, mask=mask):
            order[count] = mask

        count = count + owned.astype(jnp.int32)

    def place_of(step):
        return lax.rem(first // tile + step, depth)

    def weight_copies(step):
        at = place_of(step)
        cols = pl.ds(pl.multiple_of(first + step * tile, 128), tile)
        return [
            pltpu.make_async_copy(w.at[:, cols], ring.at[at, pl.ds(i * hid, hid)], wsem.at[at, i])
            for i, w in enumerate((w_gate, w_up))
        ]

    def row_copies(place):
        at = pl.ds(pl.multiple_of(block_of(order[place]) * BLOCK, BLOCK), BLOCK)
        return [
            pltpu.make_async_copy(a.at[at], abuf.at[place, i], asem.at[place, i])
            for i, a in enumerate(rows)
        ]

    def prepare_block(place, carry):
        for copy in row_copies(place):
            copy.wait()

        def rows_at(i, carry):
            at = pl.ds(pl.multiple_of(i * 16, 16), 16)
            grad_gate, grad_up = swiglu_grads(*(abuf[place, k, at] for k in range(3)))
            to = place * BLOCK + lax.rem(i * 16 + pair * HALF, BLOCK)
            to = pl.ds(pl.multiple_of(to, 16), 16)
            lhs[to, :hid] = grad_gate
            lhs[to, hid:] = grad_up
            return carry

        return lax.fori_loop(0, BLOCK // 16, rows_at, carry)

    def multiply(step, base, size):
        cols = pl.ds(pl.multiple_of(step * tile, tile), tile)
        out = jnp.dot(
            lhs[pl.ds(pl.multiple_of(base * BLOCK, BLOCK), size * BLOCK)],
            ring[place_of(step)],
            preferred_element_type=jnp.float32,
        ).astype(jnp.bfloat16)
        for i in range(size):
            slot = slot_of(order[base + i])
            keep[slot, :, cols] = out[i * BLOCK : i * BLOCK + HALF]
            for low, high, send in sends:

                @pl.when((slot >= low) & (slot < high))
                def _(low=low, send=send, slot=slot, i=i):
                    send[slot - low, :, cols] = out[i * BLOCK + HALF : (i + 1) * BLOCK]

    def one_tile(step, carry):
        @pl.when(step >= ahead)
        def _():
            for copy in weight_copies(step):
                copy.wait()

        def two(i, carry):
            multiply(step, 2 * i, 2)
            return carry

        lax.fori_loop(0, lax.div(count, 2), two, 0)

        @pl.when(lax.rem(count, 2) == 1)
        def _():
            multiply(step, count - 1, 1)

        @pl.when(step + depth < wanted)
        def _():
            for copy in weight_copies(step + depth):
                copy.start()

        return carry

    @pl.when(count > 0)
    def _():
        if prepare:

            def start_rows(place, carry):
                for copy in row_copies(place):
                    copy.start()
                return carry

            lax.fori_loop(0, count, start_rows, 0)
        for step in range(ahead, 1 if prepare else min(depth, wanted)):
            for copy in weight_copies(step):
                copy.start()

    for mask in range(blocks):

        @pl.when(layout[0, block_of(mask)] != mine)
        def _(slot=(mask % 2 * 2 + mask // 2) if turned else mask):
            keep[slot] = jnp.zeros_like(keep[slot])
            for low, high, send in sends:
                if low <= slot < high:
                    send[slot - low] = jnp.zeros_like(send[slot - low])

    @pl.when(count > 0)
    def _():
        if prepare:
            lax.fori_loop(0, count, prepare_block, 0)
            for step in range(1, min(depth, wanted)):
                for copy in weight_copies(step):
                    copy.start()
        lax.fori_loop(0, steps, one_tile, 0)
        for step in range(steps, wanted):
            for copy in weight_copies(step):
                copy.wait()


def terms(layout, rows, w_gate, w_up, first, width, xor, turned, waits=()):
    prepare = len(rows) == 3
    blocks = layout.shape[1]
    hid, columns = w_gate.shape
    tile = columns // sum(PLAN)
    parts = [(0, blocks)] + parts_of(blocks, xor)
    hbm_spec = pl.BlockSpec(memory_space=HBM)
    vmem_spec = pl.BlockSpec(memory_space=VMEM)
    out_shape = [pltpu.VMEM((DEPTH, 2 * hid, tile), jnp.bfloat16)]
    out_shape += [jax.ShapeDtypeStruct((b - a, HALF, width), jnp.bfloat16) for a, b in parts]
    scratch = [pltpu.SMEM((blocks,), jnp.int32), pltpu.SemaphoreType.DMA((DEPTH, 2))]
    if prepare:
        out_shape.append(pltpu.VMEM((blocks * BLOCK, 2 * hid), jnp.bfloat16))
        scratch.append(pltpu.VMEM((blocks, 3, BLOCK, hid), jnp.bfloat16))
        scratch.append(pltpu.SemaphoreType.DMA((blocks, 3)))
    constrain = pltpu.with_memory_space_constraint
    rows = [constrain(r, HBM if prepare else VMEM) for r in rows]
    return pl.pallas_call(
        functools.partial(
            terms_kernel, first=first, prepare=prepare, waits=len(waits), xor=xor, turned=turned
        ),
        in_specs=[pl.BlockSpec(memory_space=pltpu.MemorySpace.SMEM)]
        + ([hbm_spec] * 3 if prepare else [vmem_spec] * 2)
        + [hbm_spec] * 2
        + [pl.BlockSpec(memory_space=pl.ANY)] * len(waits),
        out_specs=[vmem_spec] * len(out_shape),
        out_shape=out_shape,
        scratch_shapes=scratch,
        input_output_aliases={} if prepare else {2: 0},
        compiler_params=pltpu.CompilerParams(vmem_limit_bytes=24 * 2**20),
        cost_estimate=pl.CostEstimate(
            flops=2 * blocks * BLOCK * 2 * hid * width,
            bytes_accessed=4 * hid * width,
            transcendentals=0,
        ),
        name="terms",
    )(layout, *rows, constrain(w_gate, HBM), constrain(w_up, HBM), *waits)


def swapped(x, axis, mask):
    return lax.ppermute(x, axis, [(i, i ^ mask) for i in range(lax.axis_size(axis))])


def passed_along(x, axis, by):
    size = lax.axis_size(axis)
    return lax.ppermute(x, axis, [(i, (i + by) % size) for i in range(size)])


def chunk_widths(width):
    unit = width // sum(PLAN)
    return [unit * n for n in PLAN]


def wide(x):
    return x.astype(jnp.float32)


def narrow(x):
    return x.astype(jnp.bfloat16)


def after(x, arrays):
    for a in arrays:
        a = a.reshape((-1,) + a.shape[-2:])[0, : x.shape[-2], : x.shape[-1]]
        short = [(0, n - m) for n, m in zip(x.shape[-2:], a.shape)]
        x = x + 0 * jnp.pad(a, short)
    return x


class Chunk:
    def __init__(self, keep, sends, turned, xor, waits):
        self.keep, self.turned, self.xor = keep, turned, xor
        self.other = []
        for i, send in enumerate(sends):
            other = swapped(after(send, waits) if i == 1 else send, "tensor", 1)
            self.other += [other[i] for i in range(other.shape[0])]

    def pair(self, slot):
        return wide(self.keep[slot]) + wide(self.other[slot])

    def first_half(self):
        if self.xor:
            self.far = narrow(jnp.stack([self.pair(2), self.pair(3)]))
            self.near = swapped(self.far, "dp", 1 if self.turned else 2)
        else:
            self.far = narrow(jnp.stack([self.pair(slot) for slot in range(len(self.other))]))

    def second_half(self, waits):
        if self.xor:
            far = self.pair(1) + wide(self.near[1])
            far = narrow(after(far, [wide(a) for a in waits]))
            self.last = swapped(far, "dp", 2 if self.turned else 1)
        else:
            self.last = lax.psum_scatter(self.far, "dp", scatter_dimension=0, tiled=True)[0]

    def finish(self, waits):
        out = wide(self.last)
        if self.xor:
            out = self.pair(0) + wide(self.near[0]) + out
        self.sum = narrow(after(out, [wide(a) for a in waits]))
        self.out = passed_along(self.sum, "section", -1)


def per_device(grad_hidden, gate_pre, up_pre, w_gate, w_up, block_expert):
    xor = lax.axis_size("dp") == 4
    widths = chunk_widths(w_gate.shape[2])
    rows = [grad_hidden[0], gate_pre[0], up_pre[0]]
    chunks, waits = [], []
    first = 0
    for c, width in enumerate(widths):
        turned = xor and TURNED
        ring, keep, *rest = terms(
            block_expert, rows, w_gate[0], w_up[0], first, width, xor, turned, waits
        )
        first += width
        parts = len(parts_of(keep.shape[0], xor))
        packed = rest[parts] if c == 0 else rows[0]
        rows = [packed, ring]
        ready = [chunk.out for chunk in chunks[:-2][-1:]] + [chunk.last for chunk in chunks[:-1][-1:]]
        if xor and c + 1 < len(widths):
            ready += [chunk.near for chunk in chunks[-1:]]
        chunks.append(Chunk(keep, rest[:parts], turned, xor, ready))
        chunks[c].first_half()
        if c >= 1:
            chunks[c - 1].second_half([keep])
        if c >= 2:
            chunks[c - 2].finish([keep])
        waits = [chunks[c].far]
    chunks[-1].second_half([chunks[-3].out])
    for chunk in chunks[-2:]:
        chunk.finish([])
    return jnp.concatenate([chunk.out for chunk in chunks], axis=1)[None]


def solution(mesh):
    return jax.shard_map(
        per_device,
        mesh=mesh,
        in_specs=(
            P("section", None, ("dp", "tensor")),
            P("section", None, ("dp", "tensor")),
            P("section", None, ("dp", "tensor")),
            P("section", ("dp", "tensor"), None),
            P("section", ("dp", "tensor"), None),
            P("section", None),
        ),
        out_specs=P("section", ("dp", "tensor"), None),
        check_vma=False,
    )
```

```python
import functools

import jax
import jax.numpy as jnp
from jax import lax
from jax.experimental import pallas as pl
from jax.experimental.pallas import tpu as pltpu
from jax.sharding import PartitionSpec as P

F = 8192
BLOCK = 128
HALF = BLOCK // 2
DEPTH = 3
PLAN = (3, 4, 3, 2)
HBM = pltpu.MemorySpace.HBM
VMEM = pltpu.MemorySpace.VMEM


def swiglu_grads(grad, gate, up):
    grad = grad.astype(jnp.float32)
    gate = gate.astype(jnp.float32)
    up = up.astype(jnp.float32)
    sig = 0.5 * jnp.tanh(0.5 * gate) + 0.5
    gated = gate * sig
    grad_gate = (grad * sig) * up * (1.0 + gate - gated)
    return grad_gate.astype(jnp.bfloat16), (grad * gated).astype(jnp.bfloat16)


def parts_of(blocks, xor):
    return [(0, 2), (2, 3), (3, 4)] if xor else [(0, blocks)]


def terms_kernel(*refs, first, after_width, prepare, waits, xor):
    refs = list(refs)
    layout = refs.pop(0)
    rows = [refs.pop(0) for _ in range(3 if prepare else 1)]
    if not prepare:
        refs.pop(0)
    w_gate, w_up = refs.pop(0), refs.pop(0)
    del refs[:waits]
    ring = refs.pop(0)
    keep = refs.pop(0)
    blocks, _, width = keep.shape
    sends = [(low, high, refs.pop(0)) for low, high in parts_of(blocks, xor)]
    lhs = refs.pop(0) if prepare else rows[0]
    order, wsem = refs.pop(0), refs.pop(0)
    if prepare:
        abuf, asem = refs
    hid, columns = w_gate.shape
    depth, _, tile = ring.shape
    steps = width // tile
    ahead = 0 if prepare else 1
    wanted = steps + (1 if after_width else 0)
    part = tile // 2
    rank = lax.axis_index("dp")
    pair = lax.axis_index("tensor")
    mine = lax.div((rank * lax.axis_size("tensor") + pair) * hid, F)

    def block_of(mask):
        return lax.bitwise_xor(rank, mask) if xor else mask

    def slot_of(mask, side):
        return mask % 2 * 2 + mask // 2 if xor and side else mask

    count = jnp.int32(0)
    for mask in range(blocks):
        owned = layout[0, block_of(mask)] == mine

        @pl.when(owned)
        def _(count=count, mask=mask):
            order[count] = mask

        count = count + owned.astype(jnp.int32)

    def place_of(step):
        return lax.rem(first // tile + step, depth)

    def weight_copies(step):
        at = place_of(step)
        if isinstance(step, int) and step == steps:
            start, across = first + width, after_width // 2
        else:
            start, across = first + step * part, width // 2
        return [
            pltpu.make_async_copy(
                w.at[:, pl.ds(pl.multiple_of(start + side * across, 128), part)],
                ring.at[at, pl.ds(i * hid, hid), pl.ds(side * part, part)],
                wsem.at[at, 2 * i + side],
            )
            for i, w in enumerate((w_gate, w_up))
            for side in range(2)
        ]

    def row_copies(place):
        at = pl.ds(pl.multiple_of(block_of(order[place]) * BLOCK, BLOCK), BLOCK)
        return [
            pltpu.make_async_copy(a.at[at], abuf.at[place, i], asem.at[place, i])
            for i, a in enumerate(rows)
        ]

    def prepare_block(place, carry):
        for copy in row_copies(place):
            copy.wait()

        def rows_at(i, carry):
            at = pl.ds(pl.multiple_of(i * 16, 16), 16)
            grad_gate, grad_up = swiglu_grads(*(abuf[place, k, at] for k in range(3)))
            to = place * BLOCK + lax.rem(i * 16 + pair * HALF, BLOCK)
            to = pl.ds(pl.multiple_of(to, 16), 16)
            lhs[to, :hid] = grad_gate
            lhs[to, hid:] = grad_up
            return carry

        return lax.fori_loop(0, BLOCK // 16, rows_at, carry)

    def multiply(step, base, size):
        out = jnp.dot(
            lhs[pl.ds(pl.multiple_of(base * BLOCK, BLOCK), size * BLOCK)],
            ring[place_of(step)],
            preferred_element_type=jnp.float32,
        ).astype(jnp.bfloat16)
        for i in range(size):
            for side in range(2):
                slot = slot_of(order[base + i], side)
                cols = pl.ds(pl.multiple_of(side * (width // 2) + step * part, 128), part)
                mine_out, other_out = (
                    out[i * BLOCK + k * HALF : i * BLOCK + (k + 1) * HALF, side * part : side * part + part]
                    for k in range(2)
                )
                keep[slot, :, cols] = mine_out
                for low, high, send in sends:

                    @pl.when((slot >= low) & (slot < high))
                    def _(low=low, send=send, slot=slot, cols=cols, other_out=other_out):
                        send[slot - low, :, cols] = other_out

    def one_tile(step, carry):
        @pl.when(step >= ahead)
        def _():
            for copy in weight_copies(step):
                copy.wait()

        def two(i, carry):
            multiply(step, 2 * i, 2)
            return carry

        lax.fori_loop(0, lax.div(count, 2), two, 0)

        @pl.when(lax.rem(count, 2) == 1)
        def _():
            multiply(step, count - 1, 1)

        @pl.when(step + depth < steps)
        def _():
            for copy in weight_copies(step + depth):
                copy.start()

        @pl.when(step + depth == steps)
        def _():
            if after_width:
                for copy in weight_copies(steps):
                    copy.start()

        return carry

    @pl.when(count > 0)
    def _():
        if prepare:

            def start_rows(place, carry):
                for copy in row_copies(place):
                    copy.start()
                return carry

            lax.fori_loop(0, count, start_rows, 0)
        for step in range(ahead, 1 if prepare else min(depth, wanted)):
            for copy in weight_copies(step):
                copy.start()

    for mask in range(blocks):

        @pl.when(layout[0, block_of(mask)] != mine)
        def _(mask=mask):
            for side in range(2):
                slot = slot_of(mask, side)
                cols = pl.ds(side * (width // 2), width // 2)
                zeros = jnp.zeros((HALF, width // 2), jnp.bfloat16)
                keep[slot, :, cols] = zeros
                for low, high, send in sends:
                    if low <= slot < high:
                        send[slot - low, :, cols] = zeros

    @pl.when(count > 0)
    def _():
        if prepare:
            lax.fori_loop(0, count, prepare_block, 0)
            for step in range(1, min(depth, wanted)):
                for copy in weight_copies(step):
                    copy.start()
        lax.fori_loop(0, steps, one_tile, 0)
        for step in range(steps, wanted):
            for copy in weight_copies(step):
                copy.wait()


def terms(layout, rows, w_gate, w_up, first, width, after_width, xor, waits=()):
    prepare = len(rows) == 3
    blocks = layout.shape[1]
    hid, columns = w_gate.shape
    tile = columns // sum(PLAN)
    parts = [(0, blocks)] + parts_of(blocks, xor)
    hbm_spec = pl.BlockSpec(memory_space=HBM)
    vmem_spec = pl.BlockSpec(memory_space=VMEM)
    out_shape = [pltpu.VMEM((DEPTH, 2 * hid, tile), jnp.bfloat16)]
    out_shape += [jax.ShapeDtypeStruct((b - a, HALF, width), jnp.bfloat16) for a, b in parts]
    scratch = [pltpu.SMEM((blocks,), jnp.int32), pltpu.SemaphoreType.DMA((DEPTH, 4))]
    if prepare:
        out_shape.append(pltpu.VMEM((blocks * BLOCK, 2 * hid), jnp.bfloat16))
        scratch.append(pltpu.VMEM((blocks, 3, BLOCK, hid), jnp.bfloat16))
        scratch.append(pltpu.SemaphoreType.DMA((blocks, 3)))
    constrain = pltpu.with_memory_space_constraint
    rows = [constrain(r, HBM if prepare else VMEM) for r in rows]
    return pl.pallas_call(
        functools.partial(
            terms_kernel,
            first=first,
            after_width=after_width,
            prepare=prepare,
            waits=len(waits),
            xor=xor,
        ),
        in_specs=[pl.BlockSpec(memory_space=pltpu.MemorySpace.SMEM)]
        + ([hbm_spec] * 3 if prepare else [vmem_spec] * 2)
        + [hbm_spec] * 2
        + [pl.BlockSpec(memory_space=pl.ANY)] * len(waits),
        out_specs=[vmem_spec] * len(out_shape),
        out_shape=out_shape,
        scratch_shapes=scratch,
        input_output_aliases={} if prepare else {2: 0},
        compiler_params=pltpu.CompilerParams(vmem_limit_bytes=24 * 2**20),
        cost_estimate=pl.CostEstimate(
            flops=2 * blocks * BLOCK * 2 * hid * width,
            bytes_accessed=4 * hid * width,
            transcendentals=0,
        ),
        name="terms",
    )(layout, *rows, constrain(w_gate, HBM), constrain(w_up, HBM), *waits)


def swapped(x, axis, mask):
    return lax.ppermute(x, axis, [(i, i ^ mask) for i in range(lax.axis_size(axis))])


def passed_along(x, axis, by):
    size = lax.axis_size(axis)
    return lax.ppermute(x, axis, [(i, (i + by) % size) for i in range(size)])


def chunk_widths(width):
    unit = width // sum(PLAN)
    return [unit * n for n in PLAN]


def wide(x):
    return x.astype(jnp.float32)


def narrow(x):
    return x.astype(jnp.bfloat16)


def after(x, arrays):
    for a in arrays:
        a = a.reshape((-1,) + a.shape[-2:])[0, : x.shape[-2], : x.shape[-1]]
        short = [(0, n - m) for n, m in zip(x.shape[-2:], a.shape)]
        x = x + 0 * jnp.pad(a, short)
    return x


class Chunk:
    def __init__(self, keep, sends, xor, waits):
        self.keep, self.xor = keep, xor
        half = keep.shape[-1] // 2
        self.sides = [(slice(0, half), 2), (slice(half, None), 1)]
        self.other = []
        for i, send in enumerate(sends):
            other = swapped(after(send, waits) if i == 1 else send, "tensor", 1)
            self.other += [other[i] for i in range(other.shape[0])]

    def pair(self, slot, cols=slice(None)):
        return wide(self.keep[slot, :, cols]) + wide(self.other[slot][:, cols])

    def first_half(self):
        if self.xor:
            self.far = [
                narrow(jnp.stack([self.pair(2, cols), self.pair(3, cols)])) for cols, _ in self.sides
            ]
            self.near = [swapped(far, "dp", bit) for far, (_, bit) in zip(self.far, self.sides)]
        else:
            slots = [self.pair(slot) for slot in range(len(self.other))]
            self.far, self.near = [narrow(jnp.stack(slots))], []

    def second_half(self, waits):
        if self.xor:
            self.last = []
            for near, (cols, bit) in zip(self.near, self.sides):
                far = after(self.pair(1, cols) + wide(near[1]), [wide(a) for a in waits])
                self.last.append(swapped(narrow(far), "dp", 3 - bit))
        else:
            self.last = [lax.psum_scatter(self.far[0], "dp", scatter_dimension=0, tiled=True)[0]]

    def finish(self, waits):
        if self.xor:
            out = [
                self.pair(0, cols) + wide(near[0]) + wide(last)
                for near, last, (cols, _) in zip(self.near, self.last, self.sides)
            ]
            self.sum = jnp.concatenate([narrow(after(o, [wide(a) for a in waits])) for o in out], axis=1)
        else:
            self.sum = self.last[0]
        self.out = passed_along(self.sum, "section", -1)


def per_device(grad_hidden, gate_pre, up_pre, w_gate, w_up, block_expert):
    xor = lax.axis_size("dp") == 4
    widths = chunk_widths(w_gate.shape[2])
    rows = [grad_hidden[0], gate_pre[0], up_pre[0]]
    chunks, waits = [], []
    first = 0
    for c, (width, after_width) in enumerate(zip(widths, widths[1:] + [0])):
        ring, keep, *rest = terms(
            block_expert, rows, w_gate[0], w_up[0], first, width, after_width, xor, waits
        )
        first += width
        parts = len(parts_of(keep.shape[0], xor))
        packed = rest[parts] if c == 0 else rows[0]
        rows = [packed, ring]
        ready = [chunks[c - 3].out] if c >= 3 else []
        ready += chunks[c - 2].last if c >= 2 else []
        ready += chunks[c - 1].near if c >= 1 and after_width else []
        chunks.append(Chunk(keep, rest[:parts], xor, ready))
        chunks[c].first_half()
        if c >= 1:
            chunks[c - 1].second_half([keep])
        if c >= 2:
            chunks[c - 2].finish([keep])
        waits = chunks[c].far + ([chunks[c - 2].sum] if c >= 2 else [])
    chunks[-1].second_half([chunks[-3].out])
    chunks[-2].finish(chunks[-1].far[:1])
    chunks[-1].finish([])
    return jnp.concatenate([chunk.out for chunk in chunks], axis=1)[None]


def solution(mesh):
    return jax.shard_map(
        per_device,
        mesh=mesh,
        in_specs=(
            P("section", None, ("dp", "tensor")),
            P("section", None, ("dp", "tensor")),
            P("section", None, ("dp", "tensor")),
            P("section", ("dp", "tensor"), None),
            P("section", ("dp", "tensor"), None),
            P("section", None),
        ),
        out_specs=P("section", ("dp", "tensor"), None),
        check_vma=False,
    )
```

```python
import functools

import jax
import jax.numpy as jnp
from jax import lax
from jax.experimental import pallas as pl
from jax.experimental.pallas import tpu as pltpu
from jax.sharding import PartitionSpec as P

F = 8192
BLOCK = 128
HALF = BLOCK // 2
DEPTH = 3
PLAN = (3, 4, 3, 2)
HBM = pltpu.MemorySpace.HBM
VMEM = pltpu.MemorySpace.VMEM


def swiglu_grads(grad, gate, up):
    grad = grad.astype(jnp.float32)
    gate = gate.astype(jnp.float32)
    up = up.astype(jnp.float32)
    sig = 0.5 * jnp.tanh(0.5 * gate) + 0.5
    gated = gate * sig
    grad_gate = (grad * sig) * up * (1.0 + gate - gated)
    return grad_gate.astype(jnp.bfloat16), (grad * gated).astype(jnp.bfloat16)


def parts_of(blocks, xor):
    return [(0, 2), (2, 3), (3, 4)] if xor else [(0, blocks)]


def terms_kernel(*refs, first, after_width, prepare, waits, xor):
    refs = list(refs)
    layout = refs.pop(0)
    rows = [refs.pop(0) for _ in range(3 if prepare else 1)]
    if not prepare:
        refs.pop(0)
    w_gate, w_up = refs.pop(0), refs.pop(0)
    del refs[:waits]
    ring = refs.pop(0)
    keep = refs.pop(0)
    blocks, _, width = keep.shape
    sends = [(low, high, refs.pop(0)) for low, high in parts_of(blocks, xor)]
    lhs = refs.pop(0) if prepare else rows[0]
    order, wsem = refs.pop(0), refs.pop(0)
    if prepare:
        abuf, asem = refs
    hid, columns = w_gate.shape
    depth, _, tile = ring.shape
    steps = width // tile
    ahead = 0 if prepare else 1
    wanted = steps + (1 if after_width else 0)
    part = tile // 2
    rank = lax.axis_index("dp")
    pair = lax.axis_index("tensor")
    mine = lax.div((rank * lax.axis_size("tensor") + pair) * hid, F)

    def block_of(mask):
        return lax.bitwise_xor(rank, mask) if xor else mask

    def slot_of(mask, side):
        return mask % 2 * 2 + mask // 2 if xor and side else mask

    count = jnp.int32(0)
    for mask in range(blocks):
        owned = layout[0, block_of(mask)] == mine

        @pl.when(owned)
        def _(count=count, mask=mask):
            order[count] = mask

        count = count + owned.astype(jnp.int32)

    def place_of(step):
        return lax.rem(first // tile + step, depth)

    def weight_copies(step):
        at = place_of(step)
        if isinstance(step, int) and step == steps:
            start, across = first + width, after_width // 2
        else:
            start, across = first + step * part, width // 2
        return [
            pltpu.make_async_copy(
                w.at[:, pl.ds(pl.multiple_of(start + side * across, 128), part)],
                ring.at[at, pl.ds(i * hid, hid), pl.ds(side * part, part)],
                wsem.at[at, 2 * i + side],
            )
            for i, w in enumerate((w_gate, w_up))
            for side in range(2)
        ]

    def row_copies(place):
        at = pl.ds(pl.multiple_of(block_of(order[place]) * BLOCK, BLOCK), BLOCK)
        return [
            pltpu.make_async_copy(a.at[at], abuf.at[place, i], asem.at[place, i])
            for i, a in enumerate(rows)
        ]

    def prepare_block(place, carry):
        for copy in row_copies(place):
            copy.wait()

        def rows_at(i, carry):
            at = pl.ds(pl.multiple_of(i * 16, 16), 16)
            grad_gate, grad_up = swiglu_grads(*(abuf[place, k, at] for k in range(3)))
            to = place * BLOCK + lax.rem(i * 16 + pair * HALF, BLOCK)
            to = pl.ds(pl.multiple_of(to, 16), 16)
            lhs[to, :hid] = grad_gate
            lhs[to, hid:] = grad_up
            return carry

        return lax.fori_loop(0, BLOCK // 16, rows_at, carry, unroll=2)

    def multiply(step, base, size):
        out = jnp.dot(
            lhs[pl.ds(pl.multiple_of(base * BLOCK, BLOCK), size * BLOCK)],
            ring[place_of(step)],
            preferred_element_type=jnp.float32,
        ).astype(jnp.bfloat16)
        for i in range(size):
            for side in range(2):
                slot = slot_of(order[base + i], side)
                cols = pl.ds(pl.multiple_of(side * (width // 2) + step * part, 128), part)
                mine_out, other_out = (
                    out[i * BLOCK + k * HALF : i * BLOCK + (k + 1) * HALF, side * part : side * part + part]
                    for k in range(2)
                )
                keep[slot, :, cols] = mine_out
                for low, high, send in sends:

                    @pl.when((slot >= low) & (slot < high))
                    def _(low=low, send=send, slot=slot, cols=cols, other_out=other_out):
                        send[slot - low, :, cols] = other_out

    def one_tile(step, carry):
        @pl.when(step >= ahead)
        def _():
            for copy in weight_copies(step):
                copy.wait()

        def two(i, carry):
            multiply(step, 2 * i, 2)
            return carry

        lax.fori_loop(0, lax.div(count, 2), two, 0)

        @pl.when(lax.rem(count, 2) == 1)
        def _():
            multiply(step, count - 1, 1)

        @pl.when(step + depth < steps)
        def _():
            for copy in weight_copies(step + depth):
                copy.start()

        @pl.when(step + depth == steps)
        def _():
            if after_width:
                for copy in weight_copies(steps):
                    copy.start()

        return carry

    @pl.when(count > 0)
    def _():
        if prepare:

            def start_rows(place, carry):
                for copy in row_copies(place):
                    copy.start()
                return carry

            lax.fori_loop(0, count, start_rows, 0)
        for step in range(ahead, 1 if prepare else min(depth, wanted)):
            for copy in weight_copies(step):
                copy.start()

    for mask in range(blocks):

        @pl.when(layout[0, block_of(mask)] != mine)
        def _(mask=mask):
            for side in range(2):
                slot = slot_of(mask, side)
                cols = pl.ds(side * (width // 2), width // 2)
                zeros = jnp.zeros((HALF, width // 2), jnp.bfloat16)
                keep[slot, :, cols] = zeros
                for low, high, send in sends:
                    if low <= slot < high:
                        send[slot - low, :, cols] = zeros

    @pl.when(count > 0)
    def _():
        if prepare:
            lax.fori_loop(0, count, prepare_block, 0)
            for step in range(1, min(depth, wanted)):
                for copy in weight_copies(step):
                    copy.start()
        lax.fori_loop(0, steps, one_tile, 0)
        for step in range(steps, wanted):
            for copy in weight_copies(step):
                copy.wait()


def terms(layout, rows, w_gate, w_up, first, width, after_width, xor, waits=()):
    prepare = len(rows) == 3
    blocks = layout.shape[1]
    hid, columns = w_gate.shape
    tile = columns // sum(PLAN)
    parts = [(0, blocks)] + parts_of(blocks, xor)
    hbm_spec = pl.BlockSpec(memory_space=HBM)
    vmem_spec = pl.BlockSpec(memory_space=VMEM)
    out_shape = [pltpu.VMEM((DEPTH, 2 * hid, tile), jnp.bfloat16)]
    out_shape += [jax.ShapeDtypeStruct((b - a, HALF, width), jnp.bfloat16) for a, b in parts]
    scratch = [pltpu.SMEM((blocks,), jnp.int32), pltpu.SemaphoreType.DMA((DEPTH, 4))]
    if prepare:
        out_shape.append(pltpu.VMEM((blocks * BLOCK, 2 * hid), jnp.bfloat16))
        scratch.append(pltpu.VMEM((blocks, 3, BLOCK, hid), jnp.bfloat16))
        scratch.append(pltpu.SemaphoreType.DMA((blocks, 3)))
    constrain = pltpu.with_memory_space_constraint
    rows = [constrain(r, HBM if prepare else VMEM) for r in rows]
    return pl.pallas_call(
        functools.partial(
            terms_kernel,
            first=first,
            after_width=after_width,
            prepare=prepare,
            waits=len(waits),
            xor=xor,
        ),
        in_specs=[pl.BlockSpec(memory_space=pltpu.MemorySpace.SMEM)]
        + ([hbm_spec] * 3 if prepare else [vmem_spec] * 2)
        + [hbm_spec] * 2
        + [pl.BlockSpec(memory_space=pl.ANY)] * len(waits),
        out_specs=[vmem_spec] * len(out_shape),
        out_shape=out_shape,
        scratch_shapes=scratch,
        input_output_aliases={} if prepare else {2: 0},
        compiler_params=pltpu.CompilerParams(vmem_limit_bytes=24 * 2**20),
        cost_estimate=pl.CostEstimate(
            flops=2 * blocks * BLOCK * 2 * hid * width,
            bytes_accessed=4 * hid * width,
            transcendentals=0,
        ),
        name="terms",
    )(layout, *rows, constrain(w_gate, HBM), constrain(w_up, HBM), *waits)


def swapped(x, axis, mask):
    return lax.ppermute(x, axis, [(i, i ^ mask) for i in range(lax.axis_size(axis))])


def passed_along(x, axis, by):
    size = lax.axis_size(axis)
    return lax.ppermute(x, axis, [(i, (i + by) % size) for i in range(size)])


def chunk_widths(width):
    unit = width // sum(PLAN)
    return [unit * n for n in PLAN]


def wide(x):
    return x.astype(jnp.float32)


def narrow(x):
    return x.astype(jnp.bfloat16)


def after(x, arrays):
    for a in arrays:
        a = a.reshape((-1,) + a.shape[-2:])[0, : x.shape[-2], : x.shape[-1]]
        short = [(0, n - m) for n, m in zip(x.shape[-2:], a.shape)]
        x = x + 0 * jnp.pad(a, short)
    return x


class Chunk:
    def __init__(self, keep, sends, xor, waits):
        self.keep, self.xor = keep, xor
        half = keep.shape[-1] // 2
        self.sides = [(slice(0, half), 2), (slice(half, None), 1)]
        self.other = []
        for i, send in enumerate(sends):
            other = swapped(after(send, waits) if i == 1 else send, "tensor", 1)
            self.other += [other[i] for i in range(other.shape[0])]

    def pair(self, slot, cols=slice(None)):
        return wide(self.keep[slot, :, cols]) + wide(self.other[slot][:, cols])

    def first_half(self):
        if self.xor:
            self.far = [
                narrow(jnp.stack([self.pair(2, cols), self.pair(3, cols)])) for cols, _ in self.sides
            ]
            self.near = [swapped(far, "dp", bit) for far, (_, bit) in zip(self.far, self.sides)]
        else:
            slots = [self.pair(slot) for slot in range(len(self.other))]
            self.far, self.near = [narrow(jnp.stack(slots))], []

    def second_half(self, waits):
        if self.xor:
            self.last = []
            for near, (cols, bit) in zip(self.near, self.sides):
                far = after(self.pair(1, cols) + wide(near[1]), [wide(a) for a in waits])
                self.last.append(swapped(narrow(far), "dp", 3 - bit))
        else:
            self.last = [lax.psum_scatter(self.far[0], "dp", scatter_dimension=0, tiled=True)[0]]

    def finish(self, waits):
        if self.xor:
            out = [
                self.pair(0, cols) + wide(near[0]) + wide(last)
                for near, last, (cols, _) in zip(self.near, self.last, self.sides)
            ]
            self.sum = jnp.concatenate([narrow(after(o, [wide(a) for a in waits])) for o in out], axis=1)
        else:
            self.sum = self.last[0]
        self.out = passed_along(self.sum, "section", -1)


def per_device(grad_hidden, gate_pre, up_pre, w_gate, w_up, block_expert):
    xor = lax.axis_size("dp") == 4
    widths = chunk_widths(w_gate.shape[2])
    rows = [grad_hidden[0], gate_pre[0], up_pre[0]]
    chunks, waits = [], []
    first = 0
    for c, (width, after_width) in enumerate(zip(widths, widths[1:] + [0])):
        ring, keep, *rest = terms(
            block_expert, rows, w_gate[0], w_up[0], first, width, after_width, xor, waits
        )
        first += width
        parts = len(parts_of(keep.shape[0], xor))
        packed = rest[parts] if c == 0 else rows[0]
        rows = [packed, ring]
        ready = [chunks[c - 3].out] if c >= 3 else []
        ready += chunks[c - 2].last if c >= 2 else []
        ready += chunks[c - 1].near if c >= 1 and after_width else []
        chunks.append(Chunk(keep, rest[:parts], xor, ready))
        chunks[c].first_half()
        if c >= 1:
            chunks[c - 1].second_half([keep])
        if c >= 2:
            chunks[c - 2].finish([keep])
        waits = chunks[c].far + ([chunks[c - 2].sum] if c >= 2 else [])
    chunks[-1].second_half([])
    chunks[-2].finish(chunks[-1].far[:1])
    chunks[-1].finish([chunks[-3].out])
    return jnp.concatenate([chunk.out for chunk in chunks], axis=1)[None]


def solution(mesh):
    return jax.shard_map(
        per_device,
        mesh=mesh,
        in_specs=(
            P("section", None, ("dp", "tensor")),
            P("section", None, ("dp", "tensor")),
            P("section", None, ("dp", "tensor")),
            P("section", ("dp", "tensor"), None),
            P("section", ("dp", "tensor"), None),
            P("section", None),
        ),
        out_specs=P("section", ("dp", "tensor"), None),
        check_vma=False,
    )
```

```python
import functools

import jax
import jax.numpy as jnp
from jax import lax
from jax.experimental import pallas as pl
from jax.experimental.pallas import tpu as pltpu
from jax.sharding import PartitionSpec as P

F = 8192
BLOCK = 128
HALF = BLOCK // 2
DEPTH = 3
PLAN = (3, 4, 3, 2)
HBM = pltpu.MemorySpace.HBM
VMEM = pltpu.MemorySpace.VMEM


def swiglu_grads(grad, gate, up):
    grad = grad.astype(jnp.float32)
    gate = gate.astype(jnp.float32)
    up = up.astype(jnp.float32)
    sig = 0.5 * jnp.tanh(0.5 * gate) + 0.5
    gated = gate * sig
    grad_gate = (grad * sig) * up * (1.0 + gate - gated)
    return grad_gate.astype(jnp.bfloat16), (grad * gated).astype(jnp.bfloat16)


def parts_of(blocks, xor):
    return [(0, 2), (2, 3), (3, 4)] if xor else [(0, blocks)]


def terms_kernel(*refs, first, after_width, prepare, waits, xor):
    refs = list(refs)
    layout = refs.pop(0)
    rows = [refs.pop(0) for _ in range(3 if prepare else 1)]
    if not prepare:
        refs.pop(0)
    w_gate, w_up = refs.pop(0), refs.pop(0)
    del refs[:waits]
    ring = refs.pop(0)
    keep = refs.pop(0)
    blocks, _, width = keep.shape
    sends = [(low, high, refs.pop(0)) for low, high in parts_of(blocks, xor)]
    lhs = refs.pop(0) if prepare else rows[0]
    order, wsem = refs.pop(0), refs.pop(0)
    if prepare:
        abuf, asem = refs
    hid, columns = w_gate.shape
    depth, _, tile = ring.shape
    steps = width // tile
    ahead = 0 if prepare else 1
    wanted = steps + (1 if after_width else 0)
    part = tile // 2
    rank = lax.axis_index("dp")
    pair = lax.axis_index("tensor")
    mine = lax.div((rank * lax.axis_size("tensor") + pair) * hid, F)

    def block_of(mask):
        return lax.bitwise_xor(rank, mask) if xor else mask

    def slot_of(mask, side):
        return mask % 2 * 2 + mask // 2 if xor and side else mask

    count = jnp.int32(0)
    for mask in range(blocks):
        owned = layout[0, block_of(mask)] == mine

        @pl.when(owned)
        def _(count=count, mask=mask):
            order[count] = mask

        count = count + owned.astype(jnp.int32)

    def place_of(step):
        return lax.rem(first // tile + step, depth)

    def weight_copies(step):
        at = place_of(step)
        if isinstance(step, int) and step == steps:
            start, across = first + width, after_width // 2
        else:
            start, across = first + step * part, width // 2
        return [
            pltpu.make_async_copy(
                w.at[:, pl.ds(pl.multiple_of(start + side * across, 128), part)],
                ring.at[at, pl.ds(i * hid, hid), pl.ds(side * part, part)],
                wsem.at[at, 2 * i + side],
            )
            for i, w in enumerate((w_gate, w_up))
            for side in range(2)
        ]

    def row_copies(place):
        at = pl.ds(pl.multiple_of(block_of(order[place]) * BLOCK, BLOCK), BLOCK)
        return [
            pltpu.make_async_copy(a.at[at], abuf.at[place, i], asem.at[place, i])
            for i, a in enumerate(rows)
        ]

    def prepare_block(place, carry):
        for copy in row_copies(place):
            copy.wait()

        def rows_at(i, carry):
            at = pl.ds(pl.multiple_of(i * 16, 16), 16)
            grad_gate, grad_up = swiglu_grads(*(abuf[place, k, at] for k in range(3)))
            to = place * BLOCK + lax.rem(i * 16 + pair * HALF, BLOCK)
            to = pl.ds(pl.multiple_of(to, 16), 16)
            lhs[to, :hid] = grad_gate
            lhs[to, hid:] = grad_up
            return carry

        return lax.fori_loop(0, BLOCK // 16, rows_at, carry, unroll=2)

    def multiply(step, base, size):
        out = jnp.dot(
            lhs[pl.ds(pl.multiple_of(base * BLOCK, BLOCK), size * BLOCK)],
            ring[place_of(step)],
            preferred_element_type=jnp.float32,
        ).astype(jnp.bfloat16)
        for i in range(size):
            for side in range(2):
                slot = slot_of(order[base + i], side)
                cols = pl.ds(pl.multiple_of(side * (width // 2) + step * part, 128), part)
                mine_out, other_out = (
                    out[i * BLOCK + k * HALF : i * BLOCK + (k + 1) * HALF, side * part : side * part + part]
                    for k in range(2)
                )
                keep[slot, :, cols] = mine_out
                for low, high, send in sends:

                    @pl.when((slot >= low) & (slot < high))
                    def _(low=low, send=send, slot=slot, cols=cols, other_out=other_out):
                        send[slot - low, :, cols] = other_out

    def one_tile(step, carry):
        @pl.when(step >= ahead)
        def _():
            for copy in weight_copies(step):
                copy.wait()

        def four(i, carry):
            multiply(step, 4 * i, 4)
            return carry

        lax.fori_loop(0, lax.div(count, 4), four, 0)

        @pl.when(lax.rem(count, 4) >= 2)
        def _():
            multiply(step, lax.div(count, 4) * 4, 2)

        @pl.when(lax.rem(count, 2) == 1)
        def _():
            multiply(step, count - 1, 1)

        @pl.when(step + depth < steps)
        def _():
            for copy in weight_copies(step + depth):
                copy.start()

        @pl.when(step + depth == steps)
        def _():
            if after_width:
                for copy in weight_copies(steps):
                    copy.start()

        return carry

    @pl.when(count > 0)
    def _():
        if prepare:

            def start_rows(place, carry):
                for copy in row_copies(place):
                    copy.start()
                return carry

            lax.fori_loop(0, count, start_rows, 0)
        for step in range(ahead, 1 if prepare else min(depth, wanted)):
            for copy in weight_copies(step):
                copy.start()

    for mask in range(blocks):

        @pl.when(layout[0, block_of(mask)] != mine)
        def _(mask=mask):
            for side in range(2):
                slot = slot_of(mask, side)
                cols = pl.ds(side * (width // 2), width // 2)
                zeros = jnp.zeros((HALF, width // 2), jnp.bfloat16)
                keep[slot, :, cols] = zeros
                for low, high, send in sends:
                    if low <= slot < high:
                        send[slot - low, :, cols] = zeros

    @pl.when(count > 0)
    def _():
        if prepare:
            lax.fori_loop(0, count, prepare_block, 0)
            for step in range(1, min(depth, wanted)):
                for copy in weight_copies(step):
                    copy.start()
        lax.fori_loop(0, steps, one_tile, 0)
        for step in range(steps, wanted):
            for copy in weight_copies(step):
                copy.wait()


def terms(layout, rows, w_gate, w_up, first, width, after_width, xor, waits=()):
    prepare = len(rows) == 3
    blocks = layout.shape[1]
    hid, columns = w_gate.shape
    tile = columns // sum(PLAN)
    parts = [(0, blocks)] + parts_of(blocks, xor)
    hbm_spec = pl.BlockSpec(memory_space=HBM)
    vmem_spec = pl.BlockSpec(memory_space=VMEM)
    out_shape = [pltpu.VMEM((DEPTH, 2 * hid, tile), jnp.bfloat16)]
    out_shape += [jax.ShapeDtypeStruct((b - a, HALF, width), jnp.bfloat16) for a, b in parts]
    scratch = [pltpu.SMEM((blocks,), jnp.int32), pltpu.SemaphoreType.DMA((DEPTH, 4))]
    if prepare:
        out_shape.append(pltpu.VMEM((blocks * BLOCK, 2 * hid), jnp.bfloat16))
        scratch.append(pltpu.VMEM((blocks, 3, BLOCK, hid), jnp.bfloat16))
        scratch.append(pltpu.SemaphoreType.DMA((blocks, 3)))
    constrain = pltpu.with_memory_space_constraint
    rows = [constrain(r, HBM if prepare else VMEM) for r in rows]
    return pl.pallas_call(
        functools.partial(
            terms_kernel,
            first=first,
            after_width=after_width,
            prepare=prepare,
            waits=len(waits),
            xor=xor,
        ),
        in_specs=[pl.BlockSpec(memory_space=pltpu.MemorySpace.SMEM)]
        + ([hbm_spec] * 3 if prepare else [vmem_spec] * 2)
        + [hbm_spec] * 2
        + [pl.BlockSpec(memory_space=pl.ANY)] * len(waits),
        out_specs=[vmem_spec] * len(out_shape),
        out_shape=out_shape,
        scratch_shapes=scratch,
        input_output_aliases={} if prepare else {2: 0},
        compiler_params=pltpu.CompilerParams(vmem_limit_bytes=24 * 2**20),
        cost_estimate=pl.CostEstimate(
            flops=2 * blocks * BLOCK * 2 * hid * width,
            bytes_accessed=4 * hid * width,
            transcendentals=0,
        ),
        name="terms",
    )(layout, *rows, constrain(w_gate, HBM), constrain(w_up, HBM), *waits)


def swapped(x, axis, mask):
    return lax.ppermute(x, axis, [(i, i ^ mask) for i in range(lax.axis_size(axis))])


def passed_along(x, axis, by):
    size = lax.axis_size(axis)
    return lax.ppermute(x, axis, [(i, (i + by) % size) for i in range(size)])


def chunk_widths(width):
    unit = width // sum(PLAN)
    return [unit * n for n in PLAN]


def wide(x):
    return x.astype(jnp.float32)


def narrow(x):
    return x.astype(jnp.bfloat16)


def after(x, arrays):
    for a in arrays:
        a = a.reshape((-1,) + a.shape[-2:])[0, : x.shape[-2], : x.shape[-1]]
        short = [(0, n - m) for n, m in zip(x.shape[-2:], a.shape)]
        x = x + 0 * jnp.pad(a, short)
    return x


class Chunk:
    def __init__(self, keep, sends, xor, waits):
        self.keep, self.xor = keep, xor
        half = keep.shape[-1] // 2
        self.sides = [(slice(0, half), 2), (slice(half, None), 1)]
        self.other = []
        for i, send in enumerate(sends):
            other = swapped(after(send, waits) if i == 1 else send, "tensor", 1)
            self.other += [other[i] for i in range(other.shape[0])]

    def pair(self, slot, cols=slice(None)):
        return wide(self.keep[slot, :, cols]) + wide(self.other[slot][:, cols])

    def first_half(self):
        if self.xor:
            self.far = [
                narrow(jnp.stack([self.pair(2, cols), self.pair(3, cols)])) for cols, _ in self.sides
            ]
            self.near = [swapped(far, "dp", bit) for far, (_, bit) in zip(self.far, self.sides)]
        else:
            slots = [self.pair(slot) for slot in range(len(self.other))]
            self.far, self.near = [narrow(jnp.stack(slots))], []

    def second_half(self, waits):
        if self.xor:
            self.last = []
            for near, (cols, bit) in zip(self.near, self.sides):
                far = after(self.pair(1, cols) + wide(near[1]), [wide(a) for a in waits])
                self.last.append(swapped(narrow(far), "dp", 3 - bit))
        else:
            self.last = [lax.psum_scatter(self.far[0], "dp", scatter_dimension=0, tiled=True)[0]]

    def finish(self, waits):
        if self.xor:
            out = [
                self.pair(0, cols) + wide(near[0]) + wide(last)
                for near, last, (cols, _) in zip(self.near, self.last, self.sides)
            ]
            self.sum = jnp.concatenate([narrow(after(o, [wide(a) for a in waits])) for o in out], axis=1)
        else:
            self.sum = self.last[0]
        self.out = passed_along(self.sum, "section", -1)


def per_device(grad_hidden, gate_pre, up_pre, w_gate, w_up, block_expert):
    xor = lax.axis_size("dp") == 4
    widths = chunk_widths(w_gate.shape[2])
    rows = [grad_hidden[0], gate_pre[0], up_pre[0]]
    chunks, waits = [], []
    first = 0
    for c, (width, after_width) in enumerate(zip(widths, widths[1:] + [0])):
        ring, keep, *rest = terms(
            block_expert, rows, w_gate[0], w_up[0], first, width, after_width, xor, waits
        )
        first += width
        parts = len(parts_of(keep.shape[0], xor))
        packed = rest[parts] if c == 0 else rows[0]
        rows = [packed, ring]
        ready = [chunks[c - 3].out] if c >= 3 else []
        ready += chunks[c - 2].last if c >= 2 else []
        ready += chunks[c - 1].near if c >= 1 and after_width else []
        chunks.append(Chunk(keep, rest[:parts], xor, ready))
        chunks[c].first_half()
        if c >= 1:
            chunks[c - 1].second_half([keep])
        if c >= 2:
            chunks[c - 2].finish([keep])
        waits = chunks[c].far + ([chunks[c - 2].sum] if c >= 2 else [])
    chunks[-1].second_half([])
    chunks[-2].finish(chunks[-1].far[:1])
    chunks[-1].finish([chunks[-3].out])
    return jnp.concatenate([chunk.out for chunk in chunks], axis=1)[None]


def solution(mesh):
    return jax.shard_map(
        per_device,
        mesh=mesh,
        in_specs=(
            P("section", None, ("dp", "tensor")),
            P("section", None, ("dp", "tensor")),
            P("section", None, ("dp", "tensor")),
            P("section", ("dp", "tensor"), None),
            P("section", ("dp", "tensor"), None),
            P("section", None),
        ),
        out_specs=P("section", ("dp", "tensor"), None),
        check_vma=False,
    )
```
